512 devices in a mesh: seq: 64 (over y, z_lo, core), head: 8 (over x, z_hi).
Axes of the slice: x: 4, y: 8, z: 8 (z_hi: 2, z_lo: 4; z = z_hi * 4 + z_lo), core: 2. Of those that a mesh axis runs over, the one named last changes fastest.
Arguments:
- codes: int32 [4, 16384], P(None, 'seq'), may hold values from 0 to 1023
- delays: int32 [4], replicated, may hold values from 0 to 3
- targets: int32 [4, 16384], P(None, 'seq'), may hold values from 0 to 1023
- embed: bfloat16 [4, 1024, 2048], P(None, None, 'head'), may hold values from -3 to 3
- wqkv: bfloat16 [2048, 3, 1024], P(None, None, 'head'), may hold values from -1.9224466 to 1.9224466
- wout: bfloat16 [1024, 2048], P('head'), may hold values from -0.1875 to 0.1875
- heads_w: bfloat16 [4, 2048, 1024], P(None, 'seq', 'head'), may hold values from -6.894291 to 6.894291
Outputs:
- mixed: bfloat16 [16384, 2048], P('seq', 'head')
- loss: float32 [4, 16384], P(None, ('seq', 'head'))
The draws below stay inside these ranges and needn't reach their ends.
All inputs are finite; a program needn't handle non-finite values.
Results may differ from the reference program's by a relative error of at most 0.034.
The reference program's roundings to bfloat16 on the way count: a program that leaves them out, or rounds other values in their place, can miss the bound.
Values may be sent and summed in bfloat16 or wider, within the bound.
No kernel may reach another device: no remote copies, remote signals or barrier semaphores. Data moves between devices by JAX's collectives and lax.ppermute only.
A program may use at most 128 MiB of HBM per device.

```python
import math
import jax
import jax.numpy as jnp
import numpy as np
from jax import lax

D = 2048
HEADS = 16
HD = 64
V = 1024
BOOKS = 4
FRAMES = 16384


def base_values(key, shape):
    return jnp.clip(jax.random.normal(key, shape, jnp.float32), -6.0, 6.0)


def draw_wqkv(key, part):
    key = jax.random.fold_in(key, 11)
    first = jax.random.fold_in(key, 0)
    values = base_values(first, (D, 3, HEADS * HD))
    factor = jnp.array([2.0, 1.0, 1.0], jnp.float32)[None, :, None]
    return (values * factor / math.sqrt(D)).astype(jnp.bfloat16)


def draw_heads_w(key, part):
    key = jax.random.fold_in(key, 23)
    first, second = jax.random.split(key, 2)
    values = base_values(first, (BOOKS, D, V))
    rising = jnp.exp(math.log(3.0) * jnp.arange(V, dtype=jnp.float32) / V)
    spread = jnp.exp(jax.random.uniform(second, (BOOKS, 1, V), jnp.float32, 0.0, math.log(3.0)))
    scale = rising[None, None, :] * spread
    return (values * scale / math.sqrt(D)).astype(jnp.bfloat16)


def touch_ends(values, own_key, low, top_value):
    shape = values.shape
    place = [jax.random.randint(jax.random.fold_in(own_key, axis), (), 0, shape[axis]) for axis in range(len(shape))]
    values = values.at[tuple(place)].set(low)
    longest = shape.index(max(shape))
    place[longest] = (place[longest] + 1) % shape[longest]
    return values.at[tuple(place)].set(top_value)


def shard_levels(rng, shape, cuts, least, high):
    gain = 1.0
    for position, parts in cuts:
        steps = jax.random.uniform(jax.random.fold_in(jax.random.fold_in(rng, 6), position), (parts,), jnp.float32, least / len(cuts), high / len(cuts))
        gain = gain * jnp.repeat(jnp.exp(steps), shape[position] // parts).reshape((-1,) + (1,) * (len(shape) - 1 - position))
    return gain


def cumulative_ranks(amount, lean):
    portions = [(1 << 20) // math.isqrt(rank ** lean) + 1 for rank in range(1, amount + 1)]
    deviation = 1 + sum(portions) // (1 << 30)
    return np.cumsum(np.array([max(1, weight // deviation) for weight in portions]))


def ranked(own_key, extent, number_of, lean):
    grid = cumulative_ranks(number_of, lean)
    lot = jax.random.randint(jax.random.fold_in(own_key, 1), extent, 0, int(grid[number_of - 1]))
    standing = jnp.searchsorted(jnp.asarray(grid, jnp.int32), lot, side="right")
    return jax.random.permutation(jax.random.fold_in(own_key, 2), number_of)[standing].astype(jnp.int32)


def scatter_about(key, shape, scale, most, cuts=(), kind=jnp.bfloat16):
    values = jax.random.normal(key, shape, jnp.float32) * scale
    if len(cuts) > 0:
        values = shard_levels(key, shape, cuts, -0.22, 0.18) * values
    return jnp.clip(values, min=-most, max=most).astype(kind)


def setup_inputs(seed: int = 0) -> dict:
    arg_keys = jax.random.split(jax.random.key(seed), 8)
    codes = touch_ends(ranked(arg_keys[0], (BOOKS, FRAMES), V, 2), jax.random.fold_in(arg_keys[0], 3), 0, V - 1).astype(jnp.int32)
    delays = touch_ends(jax.random.randint(arg_keys[1], (BOOKS,), 0, 4), jax.random.fold_in(arg_keys[1], 1), 0, 3).astype(jnp.int32)
    targets = touch_ends(jax.random.randint(arg_keys[2], (BOOKS, FRAMES), 0, V), jax.random.fold_in(arg_keys[2], 1), 0, V - 1).astype(jnp.int32)
    embed = scatter_about(arg_keys[3], (BOOKS, V, D), 0.5, 3.0, ((2, 8),))
    wqkv = draw_wqkv(jax.random.fold_in(arg_keys[7], 71), 0)
    wout = scatter_about(arg_keys[5], (HEADS * HD, D), (HEADS * HD) ** -0.5, 0.1875, ((0, 8),))
    heads_w = draw_heads_w(jax.random.fold_in(arg_keys[7], 71), 0)
    return dict(codes=codes, delays=delays, targets=targets, embed=embed, wqkv=wqkv, wout=wout, heads_w=heads_w)


def normalize(rows):
    mean_sq = lax.optimization_barrier(jnp.mean(jnp.square(rows), axis=-1, keepdims=True))
    return (rows * lax.rsqrt(mean_sq + 1e-05)).astype(jnp.bfloat16)

def sinusoid(frames_f, columns, width):
    half = width // 2
    freq = jnp.exp(-math.log(10000.0) * (columns % half).astype(jnp.float32) / half)
    angle = frames_f[:, None] * freq[None, :]
    return jnp.where(columns[None, :] < half, jnp.sin(angle), jnp.cos(angle))

def reference(codes, delays, targets, embed, wqkv, wout, heads_w):
    padding = jnp.zeros((BOOKS, 3), jnp.int32)
    extended = jnp.concatenate([padding, codes], axis=1)
    frame = jnp.arange(FRAMES, dtype=jnp.int32)
    where_from = (frame[None, :] + 3 - delays[:, None]).astype(jnp.int32)
    ids = jnp.take_along_axis(extended, where_from, axis=1)
    valid = frame[None, :] >= delays[:, None]
    looked = jax.vmap(lambda table, rows: jnp.take(table, rows, axis=0))(embed, ids)
    columns = jnp.arange(D, dtype=jnp.int32)
    summed = lax.optimization_barrier(jnp.sum(jnp.where(valid[:, :, None], looked.astype(jnp.float32), 0.0), axis=0))
    summed = summed + sinusoid(frame.astype(jnp.float32), columns, D)
    x_full = summed.astype(jnp.bfloat16)
    normed = normalize(x_full.astype(jnp.float32))
    width_e = HEADS * HD
    projected = jnp.dot(normed, wqkv.reshape(D, 3 * width_e), preferred_element_type=jnp.float32)
    projected = projected.astype(jnp.bfloat16).reshape(FRAMES, 3, HEADS, HD)
    queries = projected[:, 0]
    keys = projected[:, 1].astype(jnp.float32)
    values = projected[:, 2].astype(jnp.float32)
    block = min(512, FRAMES)
    scale = 1.0 / math.sqrt(HD)

    def attend_block(number):
        begin = number * block
        q_blk = lax.dynamic_slice_in_dim(queries, begin, block, 0).astype(jnp.float32)
        scores = jnp.einsum('qhe,khe->hqk', q_blk, keys) * scale
        query_pos = begin + jnp.arange(block, dtype=jnp.int32)
        allowed = frame[None, :] <= query_pos[:, None]
        masked = jnp.where(allowed[None], scores, -1e+30)
        largest = lax.optimization_barrier(jnp.max(masked, axis=-1, keepdims=True))
        weights = jnp.where(allowed[None], jnp.exp(masked - largest), 0.0)
        totals = lax.optimization_barrier(jnp.sum(weights, axis=-1))
        product = jnp.einsum('hqk,khe->hqe', weights.astype(jnp.bfloat16).astype(jnp.float32), values)
        result = (product / totals[:, :, None]).astype(jnp.bfloat16)
        return jnp.transpose(result, (1, 0, 2)).reshape(block, width_e)
    attended = lax.map(attend_block, jnp.arange(FRAMES // block, dtype=jnp.int32)).reshape(FRAMES, width_e)
    mixed = jnp.dot(attended, wout, preferred_element_type=jnp.float32).astype(jnp.bfloat16)
    resid = (x_full.astype(jnp.float32) + mixed.astype(jnp.float32)).astype(jnp.bfloat16)
    final = normalize(resid.astype(jnp.float32))
    logits = jnp.einsum('td,kdv->tkv', final.astype(jnp.float32), heads_w.astype(jnp.float32))
    largest = lax.optimization_barrier(jnp.max(logits, axis=-1))
    lse = largest + jnp.log(lax.optimization_barrier(jnp.sum(jnp.exp(logits - largest[:, :, None]), axis=-1)))
    picked = jnp.take_along_axis(logits, jnp.transpose(targets)[:, :, None], axis=-1)[:, :, 0]
    loss = jnp.transpose(lse - picked)
    return (mixed, loss)
```

```python
import functools
import math

import jax
import jax.numpy as jnp
from jax import lax
from jax.experimental import pallas as pl
from jax.experimental.pallas import tpu as pltpu
from jax.sharding import Mesh, PartitionSpec as P

HD = 64
LOW = -1e30
BF = jnp.bfloat16
F32 = jnp.float32
SEQ = ("y", "z", "c")
HEAD = ("x", "h")
VMEM = pl.BlockSpec(memory_space=pltpu.VMEM)
SMEM = pl.BlockSpec(memory_space=pltpu.SMEM)
PARAMS = pltpu.CompilerParams(vmem_limit_bytes=48 * 1024 * 1024)


def flip(array, axis, by):
    size = lax.axis_size(axis)
    return lax.ppermute(array, axis, [(i, i ^ by) for i in range(size)])


def shift(array, axis, by):
    size = lax.axis_size(axis)
    return lax.ppermute(array, axis, [(i, (i + by) % size) for i in range(size)])


def gather(array, axis):
    size = lax.axis_size(axis)
    copies = jnp.broadcast_to(array[None], (size,) + array.shape)
    return lax.all_to_all(copies, axis, 0, 0, tiled=True)


def gather_heads(array):
    other = flip(array, "h", 1)
    low = lax.axis_index("h") == 0
    pair = jnp.stack([jnp.where(low, array, other), jnp.where(low, other, array)])
    return gather(pair, "x").reshape((8,) + array.shape)


def sinusoid(frames_f, columns, width):
    half = width // 2
    freq = jnp.exp(-math.log(10000.0) * (columns % half).astype(F32) / half)
    angle = frames_f[:, None] * freq[None, :]
    return jnp.where(columns[None, :] < half, jnp.sin(angle), jnp.cos(angle))


def project_kernel(x_ref, w_ref, q_ref, kv_ref):
    parts, _, width = x_ref.shape
    squares = 0.0
    for i in range(parts):
        xi = x_ref[i].astype(F32)
        squares = squares + jnp.sum(xi * xi, axis=-1, keepdims=True)
    r = lax.rsqrt(squares / (parts * width) + 1e-05)
    sums = [0.0, 0.0, 0.0]
    for i in range(parts):
        ni = (x_ref[i].astype(F32) * r).astype(BF)
        for j in range(3):
            sums[j] = sums[j] + jnp.dot(
                ni, w_ref[j, i * width : (i + 1) * width, :], preferred_element_type=F32
            )
    q_ref[...] = sums[0].astype(BF)
    kv_ref[:, :128] = sums[1].astype(BF)
    kv_ref[:, 128:] = sums[2].astype(BF)


def project(x8, w):
    rows = x8.shape[1]
    return pl.pallas_call(
        project_kernel,
        out_shape=(
            jax.ShapeDtypeStruct((rows, 128), BF),
            jax.ShapeDtypeStruct((rows, 256), BF),
        ),
        in_specs=[VMEM, VMEM],
        out_specs=(VMEM, VMEM),
        compiler_params=PARAMS,
        name="project",
    )(x8, w)


def attend_kernel(place_ref, q_ref, kv_ref, o_ref):
    rows = q_ref.shape[1]
    blocks = kv_ref.shape[0]
    plane = pl.program_id(0)
    mine, slot = place_ref[0], place_ref[1]
    lane = lax.broadcasted_iota(jnp.int32, (rows, 128), 1)

    def put_stats(lse):
        stats = jnp.zeros((rows, 128), F32)
        rest = list(lse)
        for part in range(3):
            for h in range(2):
                top = rest[h].astype(BF).astype(F32)
                rest[h] = rest[h] - top
                stats = jnp.where(lane == 2 * part + h, top, stats)
        turned = jnp.transpose(stats)[:16, :].astype(BF)
        o_ref[0, rows : rows + 16, :] = turned[:, :128]
        o_ref[0, rows + 16 : rows + 32, :] = turned[:, 128:]

    def compute(masked):
        q = q_ref[0] * jnp.asarray(0.125, BF)
        lse, outs = [], []
        for h in range(2):
            qh = jnp.where((lane >= 64) == (h == 1), q, jnp.zeros_like(q))
            scores = []
            for j in range(blocks):
                s = lax.dot_general(
                    qh, kv_ref[j, :, :128], (((1,), (1,)), ((), ())), preferred_element_type=F32
                )
                if masked:
                    first = (slot ^ j) * rows - slot * rows
                    row = lax.broadcasted_iota(jnp.int32, s.shape, 0)
                    col = lax.broadcasted_iota(jnp.int32, s.shape, 1)
                    s = jnp.where(col - row <= -first, s, LOW)
                scores.append(s)
            top = functools.reduce(jnp.maximum, scores)
            m = jnp.max(top, axis=-1, keepdims=True)
            total = 0.0
            acc = 0.0
            for j in range(blocks):
                p = jnp.exp(scores[j] - m)
                total = total + p
                acc = acc + jnp.dot(p.astype(BF), kv_ref[j, :, 128:], preferred_element_type=F32)
            l = jnp.sum(total, axis=-1, keepdims=True)
            outs.append(acc / l)
            lse.append(m + jnp.log(l))
        o_ref[0, :rows, :] = jnp.where(lane < 64, outs[0], outs[1]).astype(BF)
        put_stats(lse)

    @pl.when(plane < mine)
    def _():
        o_ref[0, :rows, :] = jnp.zeros((rows, 128), BF)
        put_stats([jnp.full((rows, 1), LOW, F32)] * 2)

    @pl.when(plane == mine)
    def _():
        compute(True)

    @pl.when(plane > mine)
    def _():
        compute(False)


def attend(place, q8, kv8):
    planes, rows, _ = q8.shape
    return pl.pallas_call(
        attend_kernel,
        grid_spec=pltpu.PrefetchScalarGridSpec(
            num_scalar_prefetch=1,
            grid=(planes,),
            in_specs=[
                pl.BlockSpec((1, rows, 128), lambda i, s: (i, 0, 0)),
                pl.BlockSpec(kv8.shape, lambda i, s: (0, 0, 0)),
            ],
            out_specs=pl.BlockSpec((1, rows + 32, 128), lambda i, s: (i, 0, 0)),
        ),
        out_shape=jax.ShapeDtypeStruct((planes, rows + 32, 128), BF),
        compiler_params=PARAMS,
        name="attend",
    )(place, q8, kv8)


def merge_kernel(o_ref, out_ref):
    planes = o_ref.shape[0]
    rows = out_ref.shape[0]
    lane = lax.broadcasted_iota(jnp.int32, (128, 128), 1)
    for half in range(rows // 128):
        lses = []
        for i in range(planes):
            st = o_ref[i, rows + 16 * half : rows + 16 * half + 16, :].astype(F32)
            lses.append(st[0:2] + st[2:4] + st[4:6])
        top = functools.reduce(jnp.maximum, lses)
        weights = [jnp.exp(v - top) for v in lses]
        total = functools.reduce(jnp.add, weights)
        pad = jnp.zeros((128 - 2 * planes, 128), F32)
        w = jnp.transpose(jnp.concatenate([v / total for v in weights] + [pad], axis=0))
        acc = 0.0
        for i in range(planes):
            wi = jnp.where(lane < 64, w[:, 2 * i : 2 * i + 1], w[:, 2 * i + 1 : 2 * i + 2])
            acc = acc + wi * o_ref[i, 128 * half : 128 * half + 128, :].astype(F32)
        out_ref[128 * half : 128 * half + 128, :] = acc.astype(BF)


def merge(partial):
    rows = partial.shape[1] - 32
    return pl.pallas_call(
        merge_kernel,
        out_shape=jax.ShapeDtypeStruct((rows, 128), BF),
        in_specs=[VMEM],
        out_specs=VMEM,
        compiler_params=PARAMS,
        name="merge",
    )(partial)


def tail_kernel(place_ref, att_ref, near_ref, far_ref, x_ref, hw_ref, tgt_ref, mixed_ref, stat_ref, a_s, m_s, f_s):
    parts, rows, width = x_ref.shape
    head, core = place_ref[0], place_ref[1]
    for i in range(parts):
        a_s[:, 128 * i : 128 * i + 128] = att_ref[place_ref[2 + i]]
    half = near_ref.shape[-1]
    a = a_s[...]
    for ref, which in ((near_ref, core), (far_ref, 1 - core)):
        w = ref[...].reshape(parts * 128, half)
        got = jnp.dot(a, w, preferred_element_type=F32)
        m_s[:, pl.ds(pl.multiple_of(which * half, half), half)] = got.astype(BF)
    mixed_ref[...] = m_s[:, pl.ds(pl.multiple_of(head * width, width), width)]
    squares = 0.0
    for i in range(parts):
        resid = (x_ref[i].astype(F32) + m_s[:, i * width : (i + 1) * width].astype(F32)).astype(BF)
        wide = resid.astype(F32)
        squares = squares + jnp.sum(wide * wide, axis=-1, keepdims=True)
        f_s[:, i * width : (i + 1) * width] = resid
    r = lax.rsqrt(squares / (parts * width) + 1e-05)
    f_s[...] = (f_s[...].astype(F32) * r).astype(BF)
    final = f_s[...]
    books = hw_ref.shape[1]
    lane = lax.broadcasted_iota(jnp.int32, (rows, 128), 1)
    stats = jnp.zeros((rows, 128), F32)
    for b in range(books):
        w = hw_ref[:, b].reshape(parts * width, 128)
        logits = jnp.dot(final, w, preferred_element_type=F32)
        g = jnp.max(logits, axis=-1, keepdims=True)
        s = jnp.sum(jnp.exp(logits - g), axis=-1, keepdims=True)
        hit = lane + 128 * head == tgt_ref[:, b : b + 1]
        picked = jnp.sum(jnp.where(hit, logits, 0.0), axis=-1, keepdims=True)
        stats = jnp.where(lane == b, g, stats)
        stats = jnp.where(lane == books + b, s, stats)
        stats = jnp.where(lane == 2 * books + b, picked, stats)
    stat_ref[...] = stats


def tail(place, att8, near, far, x8, hw, tgt):
    parts, rows, width = x8.shape
    return pl.pallas_call(
        tail_kernel,
        out_shape=(
            jax.ShapeDtypeStruct((rows, width), BF),
            jax.ShapeDtypeStruct((rows, 128), F32),
        ),
        in_specs=[SMEM] + [VMEM] * 6,
        out_specs=(VMEM, VMEM),
        scratch_shapes=[
            pltpu.VMEM((rows, parts * 128), BF),
            pltpu.VMEM((rows, parts * width), BF),
            pltpu.VMEM((rows, parts * width), BF),
        ],
        compiler_params=PARAMS,
        name="tail",
    )(place, att8, near, far, x8, hw, tgt)


def loss_kernel(s_ref, out_ref):
    books, share = out_ref.shape
    parts = s_ref.shape[0]
    top = s_ref[0]
    for i in range(1, parts):
        top = jnp.maximum(top, s_ref[i])
    total = 0.0
    picked = 0.0
    for i in range(parts):
        v = s_ref[i]
        total = total + jnp.exp(v - top) * pltpu.roll(v, 128 - books, 1)
        picked = picked + pltpu.roll(v, 128 - 2 * books, 1)
    loss = top + jnp.log(total) - picked
    full = jnp.concatenate([loss, jnp.zeros((128 - share, 128), F32)], axis=0)
    out_ref[...] = jnp.transpose(full)[:books, :share]


def final_loss(spread, books):
    return pl.pallas_call(
        loss_kernel,
        out_shape=jax.ShapeDtypeStruct((books, spread.shape[1]), F32),
        in_specs=[VMEM],
        out_specs=VMEM,
        name="loss",
    )(spread)


def shards(codes, delays, targets, embed, wqkv, wout, heads_w):
    books, rows = codes.shape
    vocab, width = embed.shape[1:]
    y, z, c = (lax.axis_index(a) for a in SEQ)
    x, h = (lax.axis_index(a) for a in HEAD)
    head = x * 2 + h
    slot = z * 2 + c
    first = (y * 8 + slot) * rows

    hw = lax.all_gather(heads_w, SEQ, axis=0)

    devices = lax.axis_size(SEQ)
    rim = lax.ppermute(codes[:, rows - 3 :], SEQ, [(i, i + 1) for i in range(devices - 1)])
    half = wout.shape[1] // 2
    own_half = lax.dynamic_slice_in_dim(wout, c * half, half, 1)
    pair = jnp.stack([own_half, flip(own_half, "h", 1)])
    near = jnp.concatenate([pair] + [shift(pair, "x", k) for k in (1, 2, 3)])
    far = flip(near, "c", 1)
    w3 = jnp.transpose(wqkv, (1, 0, 2))

    columns = head * width + jnp.arange(width, dtype=jnp.int32)
    local = jnp.arange(rows, dtype=jnp.int32)
    frame_pos = first + local
    pos = lax.optimization_barrier(sinusoid(frame_pos.astype(F32), columns, width * 8))

    extended = jnp.concatenate([rim, codes], axis=1)
    ids = jnp.zeros((books, rows), jnp.int32)
    for d in range(4):
        ids = jnp.where(delays[:, None] == d, extended[:, 3 - d : 3 - d + rows], ids)
    ids = jnp.where(frame_pos[None, :] >= delays[:, None], ids, -1)
    hot = (jnp.transpose(ids)[:, :, None] == jnp.arange(vocab, dtype=jnp.int32)).astype(BF)
    summed = jnp.dot(
        hot.reshape(rows, books * vocab),
        embed.reshape(books * vocab, width),
        preferred_element_type=F32,
    )
    x_part = (summed + pos).astype(BF)

    x8 = gather_heads(x_part)
    q, kv = project(x8, w3)

    q8 = gather(q, "y")
    one = flip(kv, "z", 1)
    kv2 = jnp.stack([kv, one])
    kv4 = jnp.concatenate([kv2, flip(kv2, "z", 2)])
    other = flip(kv4, "c", 1)
    kv8 = jnp.stack([kv4, other], axis=1).reshape((8,) + kv.shape)

    partial = attend(jnp.stack([y, slot]).astype(jnp.int32), q8, kv8)
    spread = lax.all_to_all(partial, "y", 0, 0, tiled=True)
    att8 = gather_heads(merge(spread))

    order = [((x - k) % 4) * 2 + (h ^ j) for k in range(4) for j in range(2)]
    place = jnp.stack([head, c] + order).astype(jnp.int32)
    mixed, stats = tail(place, att8, near, far, x8, hw, jnp.transpose(targets))
    shares = lax.all_to_all(stats.reshape(8, rows // 8, 128), HEAD, 0, 0, tiled=True)
    return (mixed, final_loss(shares, books))


def solution(mesh):
    fine = Mesh(mesh.devices.reshape(8, 4, 2, 4, 2), SEQ + HEAD)
    placed = (
        P(None, SEQ),
        P(),
        P(None, SEQ),
        P(None, None, HEAD),
        P(None, None, HEAD),
        P(HEAD, None),
        P(None, SEQ, HEAD),
    )
    return jax.shard_map(
        shards,
        mesh=fine,
        in_specs=placed,
        out_specs=(P(SEQ, HEAD), P(None, SEQ + HEAD)),
        check_vma=False,
    )
```

```python
import functools
import math

import jax
import jax.numpy as jnp
from jax import lax
from jax.experimental import pallas as pl
from jax.experimental.pallas import tpu as pltpu
from jax.sharding import Mesh, PartitionSpec as P

HD = 64
LOW = -1e30
BF = jnp.bfloat16
F32 = jnp.float32
SEQ = ("y", "z", "c")
HEAD = ("x", "h")
VMEM = pl.BlockSpec(memory_space=pltpu.VMEM)
SMEM = pl.BlockSpec(memory_space=pltpu.SMEM)
PARAMS = pltpu.CompilerParams(vmem_limit_bytes=48 * 1024 * 1024)


def cost(us):
    return pl.CostEstimate(flops=us * 10**9, bytes_accessed=us * 10**6, transcendentals=0)


def flip(array, axis, by):
    size = lax.axis_size(axis)
    return lax.ppermute(array, axis, [(i, i ^ by) for i in range(size)])


def gather(array, axis):
    size = lax.axis_size(axis)
    copies = jnp.broadcast_to(array[None], (size,) + array.shape)
    return lax.all_to_all(copies, axis, 0, 0, tiled=True)


def exchange(array, axis, by):
    other = flip(array, axis, by)
    low = lax.axis_index(axis) & by == 0
    return jnp.stack([jnp.where(low, array, other), jnp.where(low, other, array)])


def gather_heads(array):
    return gather(exchange(array, "h", 1), "x").reshape((8,) + array.shape)


def sinusoid(frames_f, columns, width):
    half = width // 2
    freq = jnp.exp(-math.log(10000.0) * (columns % half).astype(F32) / half)
    angle = frames_f[:, None] * freq[None, :]
    return jnp.where(columns[None, :] < half, jnp.sin(angle), jnp.cos(angle))


def project_kernel(x_ref, w_ref, q_ref, kv_ref):
    parts, _, width = x_ref.shape
    squares = 0.0
    for i in range(parts):
        xi = x_ref[i].astype(F32)
        squares = squares + jnp.sum(xi * xi, axis=-1, keepdims=True)
    r = lax.rsqrt(squares / (parts * width) + 1e-05)
    sums = [0.0, 0.0, 0.0]
    for i in range(parts):
        ni = (x_ref[i].astype(F32) * r).astype(BF)
        for j in range(3):
            sums[j] = sums[j] + jnp.dot(
                ni, w_ref[j, i * width : (i + 1) * width, :], preferred_element_type=F32
            )
    q_ref[...] = sums[0].astype(BF)
    kv_ref[:, :128] = sums[1].astype(BF)
    kv_ref[:, 128:] = sums[2].astype(BF)


def project(x8, w):
    rows = x8.shape[1]
    return pl.pallas_call(
        project_kernel,
        out_shape=(
            jax.ShapeDtypeStruct((rows, 128), BF),
            jax.ShapeDtypeStruct((rows, 256), BF),
        ),
        in_specs=[VMEM, VMEM],
        out_specs=(VMEM, VMEM),
        compiler_params=PARAMS,
        cost_estimate=cost(2),
        name="project",
    )(x8, w)


def attend_kernel(place_ref, q_ref, near_ref, far_ref, o_ref, v_s):
    planes, rows, _ = q_ref.shape
    order = [0, 2, 1, 3]
    step = pl.program_id(0)
    mine, slot = place_ref[0], place_ref[1]
    lane = lax.broadcasted_iota(jnp.int32, (rows, 128), 1)
    blocks = [(near_ref, j, 2 * order[j]) for j in range(4)]
    blocks += [(far_ref, j, 2 * order[j] + 1) for j in range(4)]

    @pl.when(step == 0)
    def _():
        for n, (ref, j, _) in enumerate(blocks):
            v_s[n, :, :128] = ref[j, :, 128:]
            v_s[n, :, 128:] = jnp.ones((rows, 128), BF)

    def put(i, out, lse):
        o_ref[i, :rows, :] = out
        stats = jnp.zeros((rows, 128), F32)
        rest = list(lse)
        for part in range(3):
            for h in range(2):
                top = rest[h].astype(BF).astype(F32)
                rest[h] = rest[h] - top
                stats = jnp.where(lane == 2 * part + h, top, stats)
        turned = jnp.transpose(stats)[:8, :]
        o_ref[i, rows : rows + 16, :] = jnp.concatenate(
            [turned[:, :128], turned[:, 128:]], axis=0
        ).astype(BF)

    def scores(i, h, masked):
        q = q_ref[i] * jnp.asarray(0.125, BF)
        qh = jnp.where((lane >= 64) == (h == 1), q, jnp.zeros_like(q))
        found = []
        for ref, j, change in blocks:
            s = lax.dot_general(
                qh, ref[j, :, :128], (((1,), (1,)), ((), ())), preferred_element_type=F32
            )
            if masked:
                first = (slot ^ change) * rows - slot * rows
                row = lax.broadcasted_iota(jnp.int32, s.shape, 0)
                col = lax.broadcasted_iota(jnp.int32, s.shape, 1)
                s = jnp.where(col - row <= -first, s, LOW)
            found.append(s)
        return found

    def soften(found):
        m = jnp.max(functools.reduce(jnp.maximum, found), axis=-1, keepdims=True)
        return m, [jnp.exp(s - m).astype(BF) for s in found]

    def mix(m, weights):
        acc = 0.0
        for n, p in enumerate(weights):
            acc = acc + jnp.dot(p, v_s[n], preferred_element_type=F32)
        return acc[:, :128] / acc[:, 128:], m + jnp.log(acc[:, 128:129])

    def compute(modes):
        units = [(i, h) for i in range(planes) for h in range(2) if modes[i] > 0]
        found, soft, done = {}, {}, {}
        for t in range(len(units) + 2):
            if t < len(units):
                found[t] = scores(*units[t], modes[units[t][0]] == 1)
            if 0 <= t - 1 < len(units):
                soft[t - 1] = soften(found.pop(t - 1))
            if 0 <= t - 2:
                done[units[t - 2]] = mix(*soft.pop(t - 2))
        for i in range(planes):
            if modes[i] == 0:
                put(i, jnp.zeros((rows, 128), BF), [jnp.full((rows, 1), LOW, F32)] * 2)
            else:
                (a, la), (b, lb) = done[i, 0], done[i, 1]
                put(i, jnp.where(lane < 64, a, b).astype(BF), [la, lb])

    low = step * planes

    @pl.when(low > mine)
    def _():
        compute([2] * planes)

    @pl.when(low + planes - 1 < mine)
    def _():
        compute([0] * planes)

    for k in range(planes):

        @pl.when(low + k == mine)
        def _():
            compute([0] * k + [1] + [2] * (planes - 1 - k))


def attend(place, q8, near, far):
    planes, rows, _ = q8.shape
    each = 2
    whole = pl.BlockSpec(near.shape, lambda i, s: (0, 0, 0))
    return pl.pallas_call(
        attend_kernel,
        grid_spec=pltpu.PrefetchScalarGridSpec(
            num_scalar_prefetch=1,
            grid=(planes // each,),
            in_specs=[pl.BlockSpec((each, rows, 128), lambda i, s: (i, 0, 0)), whole, whole],
            out_specs=pl.BlockSpec((each, rows + 16, 128), lambda i, s: (i, 0, 0)),
            scratch_shapes=[pltpu.VMEM((8, rows, 256), BF)],
        ),
        out_shape=jax.ShapeDtypeStruct((planes, rows + 16, 128), BF),
        compiler_params=PARAMS,
        cost_estimate=cost(14),
        name="attend",
    )(place, q8, near, far)


def merge_kernel(o_ref, out_ref):
    planes = o_ref.shape[0]
    rows = out_ref.shape[0]
    lane = lax.broadcasted_iota(jnp.int32, (128, 128), 1)
    for half in range(rows // 128):
        lses = []
        for i in range(planes):
            st = o_ref[i, rows : rows + 16, :].astype(F32)[8 * half : 8 * half + 6]
            lses.append(st[0:2] + st[2:4] + st[4:6])
        top = functools.reduce(jnp.maximum, lses)
        weights = [jnp.exp(v - top) for v in lses]
        total = functools.reduce(jnp.add, weights)
        pad = jnp.zeros((128 - 2 * planes, 128), F32)
        w = jnp.transpose(jnp.concatenate([v / total for v in weights] + [pad], axis=0))
        acc = 0.0
        for i in range(planes):
            wi = jnp.where(lane < 64, w[:, 2 * i : 2 * i + 1], w[:, 2 * i + 1 : 2 * i + 2])
            acc = acc + wi * o_ref[i, 128 * half : 128 * half + 128, :].astype(F32)
        out_ref[128 * half : 128 * half + 128, :] = acc.astype(BF)


def merge(partial):
    rows = partial.shape[1] - 16
    return pl.pallas_call(
        merge_kernel,
        out_shape=jax.ShapeDtypeStruct((rows, 128), BF),
        in_specs=[VMEM],
        out_specs=VMEM,
        compiler_params=PARAMS,
        cost_estimate=cost(1),
        name="merge",
    )(partial)


def tail_kernel(place_ref, att_ref, near_ref, far_ref, x_ref, hw_ref, tgt_ref, mixed_ref, stat_ref, a_s, m_s, f_s):
    parts, rows, width = x_ref.shape
    head, core = place_ref[0], place_ref[1]
    for i in range(parts):
        a_s[:, 128 * i : 128 * i + 128] = att_ref[i]
    half = near_ref.shape[-1]
    a = a_s[...]
    for ref, which in ((near_ref, core), (far_ref, 1 - core)):
        w = ref[...].reshape(parts * 128, half)
        got = jnp.dot(a, w, preferred_element_type=F32)
        m_s[:, pl.ds(pl.multiple_of(which * half, half), half)] = got.astype(BF)
    mixed_ref[...] = m_s[:, pl.ds(pl.multiple_of(head * width, width), width)]
    squares = 0.0
    for i in range(parts):
        resid = (x_ref[i].astype(F32) + m_s[:, i * width : (i + 1) * width].astype(F32)).astype(BF)
        wide = resid.astype(F32)
        squares = squares + jnp.sum(wide * wide, axis=-1, keepdims=True)
        f_s[:, i * width : (i + 1) * width] = resid
    r = lax.rsqrt(squares / (parts * width) + 1e-05)
    f_s[...] = (f_s[...].astype(F32) * r).astype(BF)
    final = f_s[...]
    books = hw_ref.shape[1]
    lane = lax.broadcasted_iota(jnp.int32, (rows, 128), 1)
    stats = jnp.zeros((rows, 128), F32)
    for b in range(books):
        w = hw_ref[:, b].reshape(parts * width, 128)
        logits = jnp.dot(final, w, preferred_element_type=F32)
        g = jnp.max(logits, axis=-1, keepdims=True)
        s = jnp.sum(jnp.exp(logits - g), axis=-1, keepdims=True)
        hit = lane + 128 * head == tgt_ref[:, b : b + 1]
        picked = jnp.sum(jnp.where(hit, logits, 0.0), axis=-1, keepdims=True)
        stats = jnp.where(lane == b, g, stats)
        stats = jnp.where(lane == books + b, s, stats)
        stats = jnp.where(lane == 2 * books + b, picked, stats)
    stat_ref[...] = stats


def tail(place, att8, near, far, x8, hw, tgt):
    parts, rows, width = x8.shape
    return pl.pallas_call(
        tail_kernel,
        out_shape=(
            jax.ShapeDtypeStruct((rows, width), BF),
            jax.ShapeDtypeStruct((rows, 128), F32),
        ),
        in_specs=[SMEM] + [VMEM] * 6,
        out_specs=(VMEM, VMEM),
        scratch_shapes=[
            pltpu.VMEM((rows, parts * 128), BF),
            pltpu.VMEM((rows, parts * width), BF),
            pltpu.VMEM((rows, parts * width), BF),
        ],
        compiler_params=PARAMS,
        cost_estimate=cost(6),
        name="tail",
    )(place, att8, near, far, x8, hw, tgt)


def loss_kernel(s_ref, out_ref):
    books, share = out_ref.shape
    parts = s_ref.shape[0]
    top = s_ref[0]
    for i in range(1, parts):
        top = jnp.maximum(top, s_ref[i])
    total = 0.0
    picked = 0.0
    for i in range(parts):
        v = s_ref[i]
        total = total + jnp.exp(v - top) * pltpu.roll(v, 128 - books, 1)
        picked = picked + pltpu.roll(v, 128 - 2 * books, 1)
    loss = top + jnp.log(total) - picked
    full = jnp.concatenate([loss, jnp.zeros((128 - share, 128), F32)], axis=0)
    out_ref[...] = jnp.transpose(full)[:books, :share]


def final_loss(spread, books):
    return pl.pallas_call(
        loss_kernel,
        out_shape=jax.ShapeDtypeStruct((books, spread.shape[1]), F32),
        in_specs=[VMEM],
        out_specs=VMEM,
        name="loss",
    )(spread)


def shards(codes, delays, targets, embed, wqkv, wout, heads_w):
    books, rows = codes.shape
    vocab, width = embed.shape[1:]
    y, z, c = (lax.axis_index(a) for a in SEQ)
    x, h = (lax.axis_index(a) for a in HEAD)
    head = x * 2 + h
    slot = z * 2 + c
    first = (y * 8 + slot) * rows

    devices = lax.axis_size(SEQ)
    rim = lax.ppermute(codes[:, rows - 3 :], SEQ, [(i, i + 1) for i in range(devices - 1)])
    half = wout.shape[1] // 2
    pair = exchange(lax.dynamic_slice_in_dim(wout, c * half, half, 1), "h", 1)
    near = lax.all_gather(pair, "x", axis=0).reshape(8, wout.shape[0], half)
    far = flip(near, "c", 1)
    hw = exchange(exchange(exchange(heads_w, "c", 1), "z", 1), "z", 2)
    hw, near = lax.optimization_barrier((hw, near))
    hw = lax.all_gather(hw, "y", axis=0).reshape((-1,) + heads_w.shape)
    w3 = jnp.transpose(wqkv, (1, 0, 2))

    columns = head * width + jnp.arange(width, dtype=jnp.int32)
    local = jnp.arange(rows, dtype=jnp.int32)
    frame_pos = first + local
    pos = lax.optimization_barrier(sinusoid(frame_pos.astype(F32), columns, width * 8))

    extended = jnp.concatenate([rim, codes], axis=1)
    ids = jnp.zeros((books, rows), jnp.int32)
    for d in range(4):
        ids = jnp.where(delays[:, None] == d, extended[:, 3 - d : 3 - d + rows], ids)
    ids = jnp.where(frame_pos[None, :] >= delays[:, None], ids, -1)
    hot = (jnp.transpose(ids)[:, :, None] == jnp.arange(vocab, dtype=jnp.int32)).astype(BF)
    summed = jnp.dot(
        hot.reshape(rows, books * vocab),
        embed.reshape(books * vocab, width),
        preferred_element_type=F32,
    )
    x_part = (summed + pos).astype(BF)

    x8 = gather_heads(x_part)
    q, kv = project(x8, w3)

    q8 = gather(q, "y")
    kv2 = jnp.stack([kv, flip(kv, "z", 2)])
    kv4 = jnp.concatenate([kv2, flip(kv2, "z", 1)])
    kv4_far = flip(kv4, "c", 1)

    partial = attend(jnp.stack([y, slot]).astype(jnp.int32), q8, kv4, kv4_far)
    spread = lax.all_to_all(partial, "y", 0, 0, tiled=True)
    att8 = gather_heads(merge(spread))

    place = jnp.stack([head, c]).astype(jnp.int32)
    mixed, stats = tail(place, att8, near, far, x8, hw, jnp.transpose(targets))
    shares = lax.all_to_all(stats.reshape(8, rows // 8, 128), HEAD, 0, 0, tiled=True)
    return (mixed, final_loss(shares, books))


def solution(mesh):
    fine = Mesh(mesh.devices.reshape(8, 4, 2, 4, 2), SEQ + HEAD)
    placed = (
        P(None, SEQ),
        P(),
        P(None, SEQ),
        P(None, None, HEAD),
        P(None, None, HEAD),
        P(HEAD, None),
        P(None, SEQ, HEAD),
    )
    return jax.shard_map(
        shards,
        mesh=fine,
        in_specs=placed,
        out_specs=(P(SEQ, HEAD), P(None, SEQ + HEAD)),
        check_vma=False,
    )
```

```python
import functools
import math

import jax
import jax.numpy as jnp
from jax import lax
from jax.experimental import pallas as pl
from jax.experimental.pallas import tpu as pltpu
from jax.sharding import Mesh, PartitionSpec as P

HD = 64
LOW = -1e30
BF = jnp.bfloat16
F32 = jnp.float32
SEQ = ("y", "z", "c")
HEAD = ("x", "h")
VMEM = pl.BlockSpec(memory_space=pltpu.VMEM)
SMALL = pl.CostEstimate(flops=1, bytes_accessed=1, transcendentals=0)
SMEM = pl.BlockSpec(memory_space=pltpu.SMEM)
HBM = pl.BlockSpec(memory_space=pltpu.HBM)
PARAMS = pltpu.CompilerParams(vmem_limit_bytes=48 * 1024 * 1024)


def flip(array, axis, by):
    size = lax.axis_size(axis)
    return lax.ppermute(array, axis, [(i, i ^ by) for i in range(size)])


def shift(array, axis, by):
    size = lax.axis_size(axis)
    return lax.ppermute(array, axis, [(i, (i + by) % size) for i in range(size)])


def trade(array, axis):
    return lax.all_to_all(array, axis, 0, 0, tiled=True)


def after(array, first):
    return lax.optimization_barrier((array, first))[0]


def sinusoid(frames_f, columns, width):
    half = width // 2
    freq = jnp.exp(-math.log(10000.0) * (columns % half).astype(F32) / half)
    angle = frames_f[:, None] * freq[None, :]
    return jnp.where(columns[None, :] < half, jnp.sin(angle), jnp.cos(angle))


def project_kernel(x_ref, w_ref, q_ref, kv_ref, w_s, n_s, sem):
    load = pltpu.make_async_copy(w_ref, w_s, sem)
    load.start()
    parts, _, width = x_ref.shape
    squares = 0.0
    for i in range(parts):
        xi = x_ref[i].astype(F32)
        squares = squares + jnp.sum(xi * xi, axis=-1, keepdims=True)
    r = lax.rsqrt(squares / (parts * width) + 1e-05)
    for i in range(parts):
        n_s[:, i * width : (i + 1) * width] = (x_ref[i].astype(F32) * r).astype(BF)
    load.wait()
    n = n_s[...]
    q = jnp.dot(n, w_s[0], preferred_element_type=F32).astype(BF)
    for i in range(q_ref.shape[0]):
        q_ref[i] = q
    for j in range(2):
        kv = jnp.dot(n, w_s[1 + j], preferred_element_type=F32)
        kv_ref[:, 128 * j : 128 * j + 128] = kv.astype(BF)


def project(x8, w):
    parts, rows, width = x8.shape
    return pl.pallas_call(
        project_kernel,
        out_shape=(
            pltpu.HBM((8, rows, 128), BF),
            jax.ShapeDtypeStruct((rows, 256), BF),
        ),
        in_specs=[VMEM, HBM],
        out_specs=(VMEM, VMEM),
        scratch_shapes=[
            pltpu.VMEM(w.shape, BF),
            pltpu.VMEM((rows, parts * width), BF),
            pltpu.SemaphoreType.DMA,
        ],
        compiler_params=PARAMS,
        cost_estimate=SMALL,
        name="project",
    )(x8, w)


def attend_kernel(place_ref, q_ref, near_ref, far_ref, o_ref, v_s):
    planes, rows, _ = q_ref.shape
    order = [0, 2, 1, 3]
    step = pl.program_id(0)
    mine, slot = place_ref[0], place_ref[1]
    lane = lax.broadcasted_iota(jnp.int32, (rows, 128), 1)
    blocks = [(near_ref, j, 2 * order[j]) for j in range(4)]
    blocks += [(far_ref, j, 2 * order[j] + 1) for j in range(4)]

    @pl.when(step == 0)
    def _():
        for n, (ref, j, _) in enumerate(blocks):
            v_s[n, :, :128] = ref[j, :, 128:]
            v_s[n, :, 128:] = jnp.ones((rows, 128), BF)

    def put(i, out, lse):
        o_ref[i, :rows, :] = out
        stats = jnp.zeros((rows, 128), F32)
        rest = list(lse)
        for part in range(3):
            for h in range(2):
                top = rest[h].astype(BF).astype(F32)
                rest[h] = rest[h] - top
                stats = jnp.where(lane == 2 * part + h, top, stats)
        turned = jnp.transpose(stats)[:8, :]
        o_ref[i, rows : rows + 16, :] = jnp.concatenate(
            [turned[:, :128], turned[:, 128:]], axis=0
        ).astype(BF)

    def scores(i, h, masked):
        q = q_ref[i] * jnp.asarray(0.125, BF)
        qh = jnp.where((lane >= 64) == (h == 1), q, jnp.zeros_like(q))
        found = []
        for ref, j, change in blocks:
            s = lax.dot_general(
                qh, ref[j, :, :128], (((1,), (1,)), ((), ())), preferred_element_type=F32
            )
            if masked:
                first = (slot ^ change) * rows - slot * rows
                row = lax.broadcasted_iota(jnp.int32, s.shape, 0)
                col = lax.broadcasted_iota(jnp.int32, s.shape, 1)
                s = jnp.where(col - row <= -first, s, LOW)
            found.append(s)
        return found

    def soften(found):
        m = jnp.max(functools.reduce(jnp.maximum, found), axis=-1, keepdims=True)
        return m, [jnp.exp(s - m).astype(BF) for s in found]

    def mix(m, weights):
        acc = 0.0
        for n, p in enumerate(weights):
            acc = acc + jnp.dot(p, v_s[n], preferred_element_type=F32)
        return acc[:, :128] / acc[:, 128:], m + jnp.log(acc[:, 128:129])

    def compute(modes):
        units = [(i, h) for i in range(planes) for h in range(2) if modes[i] > 0]
        found, soft, done = {}, {}, {}
        for t in range(len(units) + 2):
            if t < len(units):
                found[t] = scores(*units[t], modes[units[t][0]] == 1)
            if 0 <= t - 1 < len(units):
                soft[t - 1] = soften(found.pop(t - 1))
            if 0 <= t - 2:
                done[units[t - 2]] = mix(*soft.pop(t - 2))
        for i in range(planes):
            if modes[i] == 0:
                put(i, jnp.zeros((rows, 128), BF), [jnp.full((rows, 1), LOW, F32)] * 2)
            else:
                (a, la), (b, lb) = done[i, 0], done[i, 1]
                put(i, jnp.where(lane < 64, a, b).astype(BF), [la, lb])

    low = step * planes

    @pl.when(low > mine)
    def _():
        compute([2] * planes)

    @pl.when(low + planes - 1 < mine)
    def _():
        compute([0] * planes)

    for k in range(planes):

        @pl.when(low + k == mine)
        def _():
            compute([0] * k + [1] + [2] * (planes - 1 - k))


def attend(place, q8, near, far):
    planes, rows, _ = q8.shape
    each = 2
    whole = pl.BlockSpec(near.shape, lambda i, s: (0, 0, 0))
    return pl.pallas_call(
        attend_kernel,
        grid_spec=pltpu.PrefetchScalarGridSpec(
            num_scalar_prefetch=1,
            grid=(planes // each,),
            in_specs=[pl.BlockSpec((each, rows, 128), lambda i, s: (i, 0, 0)), whole, whole],
            out_specs=pl.BlockSpec((each, rows + 16, 128), lambda i, s: (i, 0, 0)),
            scratch_shapes=[pltpu.VMEM((8, rows, 256), BF)],
        ),
        out_shape=pltpu.HBM((planes, rows + 16, 128), BF),
        compiler_params=PARAMS,
        cost_estimate=SMALL,
        name="attend",
    )(place, q8, near, far)


def merge_kernel(o_ref, out_ref):
    planes = o_ref.shape[0]
    copies, rows, _ = out_ref.shape
    lane = lax.broadcasted_iota(jnp.int32, (128, 128), 1)
    for half in range(rows // 128):
        lses = []
        for i in range(planes):
            st = o_ref[i, rows : rows + 16, :].astype(F32)[8 * half : 8 * half + 6]
            lses.append(st[0:2] + st[2:4] + st[4:6])
        top = functools.reduce(jnp.maximum, lses)
        weights = [jnp.exp(v - top) for v in lses]
        total = functools.reduce(jnp.add, weights)
        pad = jnp.zeros((128 - 2 * planes, 128), F32)
        w = jnp.transpose(jnp.concatenate([v / total for v in weights] + [pad], axis=0))
        acc = 0.0
        for i in range(planes):
            wi = jnp.where(lane < 64, w[:, 2 * i : 2 * i + 1], w[:, 2 * i + 1 : 2 * i + 2])
            acc = acc + wi * o_ref[i, 128 * half : 128 * half + 128, :].astype(F32)
        for i in range(copies):
            out_ref[i, 128 * half : 128 * half + 128, :] = acc.astype(BF)


def merge(partial):
    rows = partial.shape[1] - 16
    return pl.pallas_call(
        merge_kernel,
        out_shape=pltpu.HBM((8, rows, 128), BF),
        in_specs=[VMEM],
        out_specs=VMEM,
        compiler_params=PARAMS,
        cost_estimate=SMALL,
        name="merge",
    )(partial)


def tail_kernel(place_ref, att_ref, x_ref, hw_ref, tgt_ref, *refs):
    near_refs, far_refs = refs[:4], refs[4:8]
    mixed_ref, stat_ref, a_s, m_s, f_s = refs[8:]
    parts, rows, width = x_ref.shape
    head, core = place_ref[0], place_ref[1]
    for i in range(parts):
        a_s[:, 128 * i : 128 * i + 128] = att_ref[place_ref[2 + i]]
    half = near_refs[0].shape[-1]
    for group, which in ((near_refs, core), (far_refs, 1 - core)):
        got = 0.0
        for k, ref in enumerate(group):
            w = ref[...].reshape(256, half)
            got = got + jnp.dot(a_s[:, 256 * k : 256 * k + 256], w, preferred_element_type=F32)
        m_s[:, pl.ds(pl.multiple_of(which * half, half), half)] = got.astype(BF)
    mixed_ref[...] = m_s[:, pl.ds(pl.multiple_of(head * width, width), width)]
    squares = 0.0
    for i in range(parts):
        resid = (x_ref[i].astype(F32) + m_s[:, i * width : (i + 1) * width].astype(F32)).astype(BF)
        wide = resid.astype(F32)
        squares = squares + jnp.sum(wide * wide, axis=-1, keepdims=True)
        f_s[:, i * width : (i + 1) * width] = resid
    r = lax.rsqrt(squares / (parts * width) + 1e-05)
    f_s[...] = (f_s[...].astype(F32) * r).astype(BF)
    final = f_s[...]
    books = tgt_ref.shape[1]
    share = hw_ref.shape[1] // 2
    lane = lax.broadcasted_iota(jnp.int32, (rows, 128), 1)
    stats = jnp.zeros((rows, 128), F32)
    for i in range(2):
        w = hw_ref[:, i * share : (i + 1) * share, :].reshape(parts * width, 256)
        both = jnp.dot(final, w, preferred_element_type=F32)
        for j in range(2):
            b = 2 * j + i
            logits = both[:, 128 * j : 128 * j + 128]
            g = jnp.max(logits, axis=-1, keepdims=True)
            s = jnp.sum(jnp.exp(logits - g), axis=-1, keepdims=True)
            hit = lane + 128 * head == tgt_ref[:, b : b + 1]
            picked = jnp.sum(jnp.where(hit, logits, 0.0), axis=-1, keepdims=True)
            stats = jnp.where(lane == b, g, stats)
            stats = jnp.where(lane == books + b, s, stats)
            stats = jnp.where(lane == 2 * books + b, picked, stats)
    stat_ref[...] = stats


def tail(place, att8, x8, hw, tgt, near, far):
    parts, rows, width = x8.shape
    return pl.pallas_call(
        tail_kernel,
        out_shape=(
            jax.ShapeDtypeStruct((rows, width), BF),
            jax.ShapeDtypeStruct((rows, 128), F32),
        ),
        in_specs=[SMEM] + [VMEM] * 12,
        out_specs=(VMEM, VMEM),
        scratch_shapes=[
            pltpu.VMEM((rows, parts * 128), BF),
            pltpu.VMEM((rows, parts * width), BF),
            pltpu.VMEM((rows, parts * width), BF),
        ],
        compiler_params=PARAMS,
        cost_estimate=SMALL,
        name="tail",
    )(place, att8, x8, hw, tgt, *near, *far)


def loss_kernel(s_ref, out_ref):
    books, share = out_ref.shape
    parts = s_ref.shape[0]
    top = s_ref[0]
    for i in range(1, parts):
        top = jnp.maximum(top, s_ref[i])
    total = 0.0
    picked = 0.0
    for i in range(parts):
        v = s_ref[i]
        total = total + jnp.exp(v - top) * pltpu.roll(v, 128 - books, 1)
        picked = picked + pltpu.roll(v, 128 - 2 * books, 1)
    loss = top + jnp.log(total) - picked
    full = jnp.concatenate([loss, jnp.zeros((128 - share, 128), F32)], axis=0)
    out_ref[...] = jnp.transpose(full)[:books, :share]


def final_loss(spread, books):
    return pl.pallas_call(
        loss_kernel,
        out_shape=jax.ShapeDtypeStruct((books, spread.shape[1]), F32),
        in_specs=[VMEM],
        out_specs=VMEM,
        cost_estimate=SMALL,
        name="loss",
    )(spread)


def shards(codes, delays, targets, embed, wqkv, wout, heads_w):
    books, rows = codes.shape
    vocab, width = embed.shape[1:]
    y, z, c = (lax.axis_index(a) for a in SEQ)
    x, h = (lax.axis_index(a) for a in HEAD)
    head = x * 2 + h
    slot = z * 2 + c
    first = (y * 8 + slot) * rows

    flat = heads_w.reshape(2, -1, heads_w.shape[-1])
    rows_here = jnp.concatenate([flat[0], flat[1]], axis=1)
    plane = trade(jnp.broadcast_to(rows_here[None], (8,) + rows_here.shape), ("z", "c"))
    devices = lax.axis_size(SEQ)
    behind = lax.ppermute(codes, SEQ, [(i, i + 1) for i in range(devices - 1)])
    w3 = jnp.transpose(wqkv, (1, 0, 2))

    columns = head * width + jnp.arange(width, dtype=jnp.int32)
    local = jnp.arange(rows, dtype=jnp.int32)
    frame_pos = first + local
    pos = lax.optimization_barrier(sinusoid(frame_pos.astype(F32), columns, width * 8))

    extended = jnp.concatenate([behind[:, rows - 3 :], codes], axis=1)
    ids = jnp.zeros((books, rows), jnp.int32)
    for d in range(4):
        ids = jnp.where(delays[:, None] == d, extended[:, 3 - d : 3 - d + rows], ids)
    ids = jnp.where(frame_pos[None, :] >= delays[:, None], ids, -1)
    hot = (jnp.transpose(ids)[:, :, None] == jnp.arange(vocab, dtype=jnp.int32)).astype(BF)
    summed = jnp.dot(
        hot.reshape(rows, books * vocab),
        embed.reshape(books * vocab, width),
        preferred_element_type=F32,
    )
    x_part = (summed + pos).astype(BF)
    x_part, plane = lax.optimization_barrier((x_part, plane))
    hw = lax.all_gather(plane, "y", axis=0).reshape((-1,) + rows_here.shape)

    other = flip(x_part, "h", 1)
    both = jnp.stack([jnp.where(h == 0, x_part, other), jnp.where(h == 0, other, x_part)])
    x8 = trade(jnp.broadcast_to(both[None], (4,) + both.shape), "x").reshape((8,) + x_part.shape)
    half = wout.shape[1] // 2
    mine = after(lax.dynamic_slice_in_dim(wout, c * half, half, 1), both)
    theirs = flip(mine, "h", 1)

    q, kv = project(x8, w3)
    q8 = trade(q, "y")
    kv2 = jnp.stack([kv, flip(kv, "z", 2)])
    kv2 = after(kv2, theirs)
    kv4 = jnp.concatenate([kv2, flip(kv2, "z", 1)])
    kv4_far = flip(kv4, "c", 1)
    partial = attend(jnp.stack([y, slot]).astype(jnp.int32), q8, kv4, kv4_far)
    pair = jnp.stack(after([mine, theirs], partial))
    near = [pair] + [shift(pair, "x", k) for k in (1, 2, 3)]

    att = merge(trade(partial, "y"))
    waits = [partial, att, att, att]
    far = [flip(after(n, first), "c", 1) for n, first in zip(near, waits)]
    att8 = trade(att, HEAD)

    order = [((x - k) % 4) * 2 + (h ^ j) for k in range(4) for j in range(2)]
    place = jnp.stack([head, c] + order).astype(jnp.int32)
    mixed, stats = tail(place, att8, x8, hw, jnp.transpose(targets), near, far)
    shares = trade(stats.reshape(8, rows // 8, 128), HEAD)
    return (mixed, final_loss(shares, books))


def solution(mesh):
    fine = Mesh(mesh.devices.reshape(8, 4, 2, 4, 2), SEQ + HEAD)
    placed = (
        P(None, SEQ),
        P(),
        P(None, SEQ),
        P(None, None, HEAD),
        P(None, None, HEAD),
        P(HEAD, None),
        P(None, SEQ, HEAD),
    )
    return jax.shard_map(
        shards,
        mesh=fine,
        in_specs=placed,
        out_specs=(P(SEQ, HEAD), P(None, SEQ + HEAD)),
        check_vma=False,
    )
```

```python
import functools
import math

import jax
import jax.numpy as jnp
from jax import lax
from jax.experimental import pallas as pl
from jax.experimental.pallas import tpu as pltpu
from jax.sharding import Mesh, PartitionSpec as P

HD = 64
LOW = -1e30
BF = jnp.bfloat16
F32 = jnp.float32
SEQ = ("y", "z", "c")
HEAD = ("x", "h")
VMEM = pl.BlockSpec(memory_space=pltpu.VMEM)
SMALL = pl.CostEstimate(flops=1, bytes_accessed=1, transcendentals=0)
SMEM = pl.BlockSpec(memory_space=pltpu.SMEM)
HBM = pl.BlockSpec(memory_space=pltpu.HBM)


def room(mib):
    return pltpu.CompilerParams(vmem_limit_bytes=mib * 1024 * 1024)


def flip(array, axis, by):
    size = lax.axis_size(axis)
    return lax.ppermute(array, axis, [(i, i ^ by) for i in range(size)])


def shift(array, axis, by):
    size = lax.axis_size(axis)
    return lax.ppermute(array, axis, [(i, (i + by) % size) for i in range(size)])


def trade(array, axis):
    return lax.all_to_all(array, axis, 0, 0, tiled=True)


def after(array, first):
    return lax.optimization_barrier((array, first))[0]


def sinusoid(frames_f, columns, width):
    half = width // 2
    freq = jnp.exp(-math.log(10000.0) * (columns % half).astype(F32) / half)
    angle = frames_f[:, None] * freq[None, :]
    return jnp.where(columns[None, :] < half, jnp.sin(angle), jnp.cos(angle))


def project_kernel(x_ref, w_ref, q_ref, kv_ref):
    parts, _, width = x_ref.shape
    squares = 0.0
    for i in range(parts):
        xi = x_ref[i].astype(F32)
        squares = squares + jnp.sum(xi * xi, axis=-1, keepdims=True)
    r = lax.rsqrt(squares / (parts * width) + 1e-05)
    sums = [0.0, 0.0, 0.0]
    for i in range(parts):
        ni = (x_ref[i].astype(F32) * r).astype(BF)
        for j in range(3):
            sums[j] = sums[j] + jnp.dot(
                ni, w_ref[j, i * width : (i + 1) * width, :], preferred_element_type=F32
            )
    q_ref[...] = sums[0].astype(BF)
    kv_ref[:, :128] = sums[1].astype(BF)
    kv_ref[:, 128:] = sums[2].astype(BF)


def project(x8, w):
    rows = x8.shape[1]
    return pl.pallas_call(
        project_kernel,
        out_shape=(
            jax.ShapeDtypeStruct((rows, 128), BF),
            jax.ShapeDtypeStruct((rows, 256), BF),
        ),
        in_specs=[VMEM, VMEM],
        out_specs=(VMEM, VMEM),
        compiler_params=room(12),
        name="project",
    )(x8, w)


def attend_kernel(place_ref, q_ref, near_ref, far_ref, o_ref, v_s):
    planes, rows, _ = q_ref.shape
    order = [0, 2, 1, 3]
    step = pl.program_id(0)
    mine, slot = place_ref[0], place_ref[1]
    lane = lax.broadcasted_iota(jnp.int32, (rows, 128), 1)
    blocks = [(near_ref, j, 2 * order[j]) for j in range(4)]
    blocks += [(far_ref, j, 2 * order[j] + 1) for j in range(4)]

    @pl.when(step == 0)
    def _():
        for n, (ref, j, _) in enumerate(blocks):
            v_s[n, :, :128] = ref[j, :, 128:]
            v_s[n, :, 128:] = jnp.ones((rows, 128), BF)

    def put(i, out, lse):
        o_ref[i, :rows, :] = out
        stats = jnp.zeros((rows, 128), F32)
        rest = list(lse)
        for part in range(3):
            for h in range(2):
                top = rest[h].astype(BF).astype(F32)
                rest[h] = rest[h] - top
                stats = jnp.where(lane == 2 * part + h, top, stats)
        turned = jnp.transpose(stats)[:8, :]
        o_ref[i, rows : rows + 16, :] = jnp.concatenate(
            [turned[:, :128], turned[:, 128:]], axis=0
        ).astype(BF)

    def scores(i, h, masked):
        q = q_ref[i] * jnp.asarray(0.125, BF)
        qh = jnp.where((lane >= 64) == (h == 1), q, jnp.zeros_like(q))
        found = []
        for ref, j, change in blocks:
            s = lax.dot_general(
                qh, ref[j, :, :128], (((1,), (1,)), ((), ())), preferred_element_type=F32
            )
            if masked:
                first = (slot ^ change) * rows - slot * rows
                row = lax.broadcasted_iota(jnp.int32, s.shape, 0)
                col = lax.broadcasted_iota(jnp.int32, s.shape, 1)
                s = jnp.where(col - row <= -first, s, LOW)
            found.append(s)
        return found

    def soften(found):
        m = jnp.max(functools.reduce(jnp.maximum, found), axis=-1, keepdims=True)
        return m, [jnp.exp(s - m).astype(BF) for s in found]

    def mix(m, weights):
        acc = 0.0
        for n, p in enumerate(weights):
            acc = acc + jnp.dot(p, v_s[n], preferred_element_type=F32)
        return acc[:, :128] / acc[:, 128:], m + jnp.log(acc[:, 128:129])

    def compute(modes):
        units = [(i, h) for i in range(planes) for h in range(2) if modes[i] > 0]
        found, soft, done = {}, {}, {}
        for t in range(len(units) + 2):
            if t < len(units):
                found[t] = scores(*units[t], modes[units[t][0]] == 1)
            if 0 <= t - 1 < len(units):
                soft[t - 1] = soften(found.pop(t - 1))
            if 0 <= t - 2:
                done[units[t - 2]] = mix(*soft.pop(t - 2))
        for i in range(planes):
            if modes[i] == 0:
                put(i, jnp.zeros((rows, 128), BF), [jnp.full((rows, 1), LOW, F32)] * 2)
            else:
                (a, la), (b, lb) = done[i, 0], done[i, 1]
                put(i, jnp.where(lane < 64, a, b).astype(BF), [la, lb])

    low = step * planes

    @pl.when(low > mine)
    def _():
        compute([2] * planes)

    @pl.when(low + planes - 1 < mine)
    def _():
        compute([0] * planes)

    for k in range(planes):

        @pl.when(low + k == mine)
        def _():
            compute([0] * k + [1] + [2] * (planes - 1 - k))


def attend(place, q8, near, far):
    planes, rows, _ = q8.shape
    each = 4
    whole = pl.BlockSpec(near.shape, lambda i, s: (0, 0, 0))
    return pl.pallas_call(
        attend_kernel,
        grid_spec=pltpu.PrefetchScalarGridSpec(
            num_scalar_prefetch=1,
            grid=(planes // each,),
            in_specs=[pl.BlockSpec((each, rows, 128), lambda i, s: (i, 0, 0)), whole, whole],
            out_specs=pl.BlockSpec((each, rows + 16, 128), lambda i, s: (i, 0, 0)),
            scratch_shapes=[pltpu.VMEM((8, rows, 256), BF)],
        ),
        out_shape=pltpu.HBM((planes, rows + 16, 128), BF),
        compiler_params=room(24),
        cost_estimate=SMALL,
        name="attend",
    )(place, q8, near, far)


def merge_kernel(o_ref, out_ref):
    planes = o_ref.shape[0]
    rows = out_ref.shape[0]
    lane = lax.broadcasted_iota(jnp.int32, (128, 128), 1)
    for half in range(rows // 128):
        lses = []
        for i in range(planes):
            st = o_ref[i, rows : rows + 16, :].astype(F32)[8 * half : 8 * half + 6]
            lses.append(st[0:2] + st[2:4] + st[4:6])
        top = functools.reduce(jnp.maximum, lses)
        weights = [jnp.exp(v - top) for v in lses]
        total = functools.reduce(jnp.add, weights)
        pad = jnp.zeros((128 - 2 * planes, 128), F32)
        w = jnp.transpose(jnp.concatenate([v / total for v in weights] + [pad], axis=0))
        acc = 0.0
        for i in range(planes):
            wi = jnp.where(lane < 64, w[:, 2 * i : 2 * i + 1], w[:, 2 * i + 1 : 2 * i + 2])
            acc = acc + wi * o_ref[i, 128 * half : 128 * half + 128, :].astype(F32)
        out_ref[128 * half : 128 * half + 128, :] = acc.astype(BF)


def merge(partial):
    rows = partial.shape[1] - 16
    return pl.pallas_call(
        merge_kernel,
        out_shape=jax.ShapeDtypeStruct((rows, 128), BF),
        in_specs=[VMEM],
        out_specs=VMEM,
        compiler_params=room(8),
        cost_estimate=SMALL,
        name="merge",
    )(partial)


def tail_kernel(place_ref, att_ref, x_ref, hw_ref, hw_far_ref, tgt_ref, *refs):
    near_refs, far_refs = refs[:4], refs[4:8]
    mixed_ref, stat_ref, a_s, m_s, f_s = refs[8:]
    parts, rows, width = x_ref.shape
    head, core = place_ref[0], place_ref[1]
    for i in range(parts):
        a_s[:, 128 * i : 128 * i + 128] = att_ref[place_ref[2 + i]]
    half = near_refs[0].shape[-1]
    for group, which in ((near_refs, core), (far_refs, 1 - core)):
        got = 0.0
        for k, ref in enumerate(group):
            w = ref[...].reshape(256, half)
            got = got + jnp.dot(a_s[:, 256 * k : 256 * k + 256], w, preferred_element_type=F32)
        m_s[:, pl.ds(pl.multiple_of(which * half, half), half)] = got.astype(BF)
    mixed_ref[...] = m_s[:, pl.ds(pl.multiple_of(head * width, width), width)]
    squares = 0.0
    for i in range(parts):
        resid = (x_ref[i].astype(F32) + m_s[:, i * width : (i + 1) * width].astype(F32)).astype(BF)
        wide = resid.astype(F32)
        squares = squares + jnp.sum(wide * wide, axis=-1, keepdims=True)
        f_s[:, i * width : (i + 1) * width] = resid
    r = lax.rsqrt(squares / (parts * width) + 1e-05)
    f_s[...] = (f_s[...].astype(F32) * r).astype(BF)
    final = f_s[...]
    books = tgt_ref.shape[1]
    share = hw_ref.shape[1] // 2
    lane = lax.broadcasted_iota(jnp.int32, (rows, 128), 1)
    stats = jnp.zeros((rows, 128), F32)
    for ref, which in ((hw_ref, core), (hw_far_ref, 1 - core)):
        for i in range(2):
            w = ref[:, i * share : (i + 1) * share, :].reshape(parts * width, 128)
            logits = jnp.dot(final, w, preferred_element_type=F32)
            b = 2 * which + i
            goal = jnp.where(which == 0, tgt_ref[:, i : i + 1], tgt_ref[:, 2 + i : 3 + i])
            g = jnp.max(logits, axis=-1, keepdims=True)
            s = jnp.sum(jnp.exp(logits - g), axis=-1, keepdims=True)
            picked = jnp.where(lane + 128 * head == goal, logits, 0.0)
            picked = jnp.sum(picked, axis=-1, keepdims=True)
            stats = jnp.where(lane == b, g, stats)
            stats = jnp.where(lane == books + b, s, stats)
            stats = jnp.where(lane == 2 * books + b, picked, stats)
    stat_ref[...] = stats


def tail(place, att8, x8, hw, hw_far, tgt, near, far):
    parts, rows, width = x8.shape
    return pl.pallas_call(
        tail_kernel,
        out_shape=(
            jax.ShapeDtypeStruct((rows, width), BF),
            jax.ShapeDtypeStruct((rows, 128), F32),
        ),
        in_specs=[SMEM] + [VMEM] * 13,
        out_specs=(VMEM, VMEM),
        scratch_shapes=[
            pltpu.VMEM((rows, parts * 128), BF),
            pltpu.VMEM((rows, parts * width), BF),
            pltpu.VMEM((rows, parts * width), BF),
        ],
        compiler_params=room(28),
        cost_estimate=SMALL,
        name="tail",
    )(place, att8, x8, hw, hw_far, tgt, *near, *far)


def loss_kernel(s_ref, out_ref):
    books, share = out_ref.shape
    parts = s_ref.shape[0]
    top = s_ref[0]
    for i in range(1, parts):
        top = jnp.maximum(top, s_ref[i])
    total = 0.0
    picked = 0.0
    for i in range(parts):
        v = s_ref[i]
        total = total + jnp.exp(v - top) * pltpu.roll(v, 128 - books, 1)
        picked = picked + pltpu.roll(v, 128 - 2 * books, 1)
    loss = top + jnp.log(total) - picked
    full = jnp.concatenate([loss, jnp.zeros((128 - share, 128), F32)], axis=0)
    out_ref[...] = jnp.transpose(full)[:books, :share]


def final_loss(spread, books):
    return pl.pallas_call(
        loss_kernel,
        out_shape=jax.ShapeDtypeStruct((books, spread.shape[1]), F32),
        in_specs=[VMEM],
        out_specs=VMEM,
        cost_estimate=SMALL,
        name="loss",
    )(spread)


def shards(codes, delays, targets, embed, wqkv, wout, heads_w):
    books, rows = codes.shape
    vocab, width = embed.shape[1:]
    y, z, c = (lax.axis_index(a) for a in SEQ)
    x, h = (lax.axis_index(a) for a in HEAD)
    head = x * 2 + h
    slot = z * 2 + c
    first = (y * 8 + slot) * rows

    halves = heads_w.reshape(1, 2, -1, heads_w.shape[-1])
    plane = trade(
        jnp.broadcast_to(halves, (4,) + halves.shape[1:]).reshape((8,) + halves.shape[2:]), ("z", "c")
    )
    devices = lax.axis_size(SEQ)
    behind = lax.ppermute(codes, SEQ, [(i, i + 1) for i in range(devices - 1)])
    w3 = jnp.transpose(wqkv, (1, 0, 2))

    columns = head * width + jnp.arange(width, dtype=jnp.int32)
    local = jnp.arange(rows, dtype=jnp.int32)
    frame_pos = first + local
    pos = lax.optimization_barrier(sinusoid(frame_pos.astype(F32), columns, width * 8))

    extended = jnp.concatenate([behind[:, rows - 3 :], codes], axis=1)
    ids = jnp.zeros((books, rows), jnp.int32)
    for d in range(4):
        ids = jnp.where(delays[:, None] == d, extended[:, 3 - d : 3 - d + rows], ids)
    ids = jnp.where(frame_pos[None, :] >= delays[:, None], ids, -1)
    hot = (jnp.transpose(ids)[:, :, None] == jnp.arange(vocab, dtype=jnp.int32)).astype(BF)
    summed = jnp.dot(
        hot.reshape(rows, books * vocab),
        embed.reshape(books * vocab, width),
        preferred_element_type=F32,
    )
    x_part = (summed + pos).astype(BF)
    x_part, plane = lax.optimization_barrier((x_part, plane))
    hw = lax.all_gather(plane, "y", axis=0).reshape((-1,) + halves.shape[2:])

    other = flip(x_part, "h", 1)
    both = jnp.stack([jnp.where(h == 0, x_part, other), jnp.where(h == 0, other, x_part)])
    x8 = trade(jnp.broadcast_to(both[None], (4,) + both.shape), "x").reshape((8,) + x_part.shape)
    half = wout.shape[1] // 2
    mine = after(lax.dynamic_slice_in_dim(wout, c * half, half, 1), both)
    theirs = flip(mine, "h", 1)

    q, kv = project(x8, w3)
    q8 = trade(jnp.broadcast_to(q[None], (8,) + q.shape), "y")
    kv2 = jnp.stack([kv, flip(kv, "z", 2)])
    kv2 = after(kv2, theirs)
    kv4 = jnp.concatenate([kv2, flip(kv2, "z", 1)])
    kv4_far = flip(kv4, "c", 1)
    partial = attend(jnp.stack([y, slot]).astype(jnp.int32), q8, kv4, kv4_far)
    pair = jnp.stack([mine, theirs])
    near = [pair] + [shift(pair, "x", k) for k in (1, 2, 3)]

    att = merge(trade(partial, "y"))
    waits = [partial, att, att, att]
    far = [flip(after(n, first), "c", 1) for n, first in zip(near, waits)]
    hw = after(hw, partial)
    hw_far = flip(hw, "c", 1)
    att8 = trade(jnp.broadcast_to(att[None], (8,) + att.shape), HEAD)

    order = [((x - k) % 4) * 2 + (h ^ j) for k in range(4) for j in range(2)]
    place = jnp.stack([head, c] + order).astype(jnp.int32)
    mixed, stats = tail(place, att8, x8, hw, hw_far, jnp.transpose(targets), near, far)
    shares = trade(stats.reshape(8, rows // 8, 128), HEAD)
    return (mixed, final_loss(shares, books))


def solution(mesh):
    fine = Mesh(mesh.devices.reshape(8, 4, 2, 4, 2), SEQ + HEAD)
    placed = (
        P(None, SEQ),
        P(),
        P(None, SEQ),
        P(None, None, HEAD),
        P(None, None, HEAD),
        P(HEAD, None),
        P(None, SEQ, HEAD),
    )
    return jax.shard_map(
        shards,
        mesh=fine,
        in_specs=placed,
        out_specs=(P(SEQ, HEAD), P(None, SEQ + HEAD)),
        check_vma=False,
    )
```

```python
import functools
import math

import jax
import jax.numpy as jnp
from jax import lax
from jax.experimental import pallas as pl
from jax.experimental.pallas import tpu as pltpu
from jax.sharding import Mesh, PartitionSpec as P

HD = 64
LOW = -1e30
BF = jnp.bfloat16
F32 = jnp.float32
SEQ = ("y", "z", "c")
HEAD = ("x", "h")
VMEM = pl.BlockSpec(memory_space=pltpu.VMEM)
SMALL = pl.CostEstimate(flops=1, bytes_accessed=1, transcendentals=0)
SMEM = pl.BlockSpec(memory_space=pltpu.SMEM)
HBM = pl.BlockSpec(memory_space=pltpu.HBM)
PARAMS = pltpu.CompilerParams(vmem_limit_bytes=48 * 1024 * 1024)


def flip(array, axis, by):
    size = lax.axis_size(axis)
    return lax.ppermute(array, axis, [(i, i ^ by) for i in range(size)])


def shift(array, axis, by):
    size = lax.axis_size(axis)
    return lax.ppermute(array, axis, [(i, (i + by) % size) for i in range(size)])


def trade(array, axis):
    return lax.all_to_all(array, axis, 0, 0, tiled=True)


def after(array, first):
    return lax.optimization_barrier((array, first))[0]


def sinusoid(frames_f, columns, width):
    half = width // 2
    freq = jnp.exp(-math.log(10000.0) * (columns % half).astype(F32) / half)
    angle = frames_f[:, None] * freq[None, :]
    return jnp.where(columns[None, :] < half, jnp.sin(angle), jnp.cos(angle))


def project_kernel(x_ref, w_ref, q_ref, kv_ref):
    parts, _, width = x_ref.shape
    squares = 0.0
    for i in range(parts):
        xi = x_ref[i].astype(F32)
        squares = squares + jnp.sum(xi * xi, axis=-1, keepdims=True)
    r = lax.rsqrt(squares / (parts * width) + 1e-05)
    sums = [0.0, 0.0, 0.0]
    for i in range(parts):
        ni = (x_ref[i].astype(F32) * r).astype(BF)
        for j in range(3):
            sums[j] = sums[j] + jnp.dot(
                ni, w_ref[j, i * width : (i + 1) * width, :], preferred_element_type=F32
            )
    q_ref[...] = sums[0].astype(BF)
    kv_ref[:, :128] = sums[1].astype(BF)
    kv_ref[:, 128:] = sums[2].astype(BF)


def project(x8, w):
    rows = x8.shape[1]
    return pl.pallas_call(
        project_kernel,
        out_shape=(
            jax.ShapeDtypeStruct((rows, 128), BF),
            jax.ShapeDtypeStruct((rows, 256), BF),
        ),
        in_specs=[VMEM, VMEM],
        out_specs=(VMEM, VMEM),
        compiler_params=PARAMS,
        name="project",
    )(x8, w)


def attend_kernel(place_ref, q_ref, near_ref, far_ref, o_ref, v_s):
    planes, rows, _ = q_ref.shape
    order = [0, 2, 1, 3]
    step = pl.program_id(0)
    mine, slot = place_ref[0], place_ref[1]
    lane = lax.broadcasted_iota(jnp.int32, (rows, 128), 1)
    blocks = [(near_ref, j, 2 * order[j]) for j in range(4)]
    blocks += [(far_ref, j, 2 * order[j] + 1) for j in range(4)]

    @pl.when(step == 0)
    def _():
        for n, (ref, j, _) in enumerate(blocks):
            v_s[n, :, :128] = ref[j, :, 128:]
            v_s[n, :, 128:] = jnp.ones((rows, 128), BF)

    def put(i, out, lse):
        o_ref[i, :rows, :] = out
        stats = jnp.zeros((rows, 128), F32)
        rest = list(lse)
        for part in range(3):
            for h in range(2):
                top = rest[h].astype(BF).astype(F32)
                rest[h] = rest[h] - top
                stats = jnp.where(lane == 2 * part + h, top, stats)
        turned = jnp.transpose(stats)[:8, :]
        o_ref[i, rows : rows + 16, :] = jnp.concatenate(
            [turned[:, :128], turned[:, 128:]], axis=0
        ).astype(BF)

    def scores(i, h, masked):
        q = q_ref[i] * jnp.asarray(0.125, BF)
        qh = jnp.where((lane >= 64) == (h == 1), q, jnp.zeros_like(q))
        found = []
        for ref, j, change in blocks:
            s = lax.dot_general(
                qh, ref[j, :, :128], (((1,), (1,)), ((), ())), preferred_element_type=F32
            )
            if masked:
                first = (slot ^ change) * rows - slot * rows
                row = lax.broadcasted_iota(jnp.int32, s.shape, 0)
                col = lax.broadcasted_iota(jnp.int32, s.shape, 1)
                s = jnp.where(col - row <= -first, s, LOW)
            found.append(s)
        return found

    def soften(found):
        m = jnp.max(functools.reduce(jnp.maximum, found), axis=-1, keepdims=True)
        return m, [jnp.exp(s - m).astype(BF) for s in found]

    def mix(m, weights):
        acc = 0.0
        for n, p in enumerate(weights):
            acc = acc + jnp.dot(p, v_s[n], preferred_element_type=F32)
        return acc[:, :128] / acc[:, 128:], m + jnp.log(acc[:, 128:129])

    def compute(modes):
        units = [(i, h) for i in range(planes) for h in range(2) if modes[i] > 0]
        found, soft, done = {}, {}, {}
        for t in range(len(units) + 2):
            if t < len(units):
                found[t] = scores(*units[t], modes[units[t][0]] == 1)
            if 0 <= t - 1 < len(units):
                soft[t - 1] = soften(found.pop(t - 1))
            if 0 <= t - 2:
                done[units[t - 2]] = mix(*soft.pop(t - 2))
        for i in range(planes):
            if modes[i] == 0:
                put(i, jnp.zeros((rows, 128), BF), [jnp.full((rows, 1), LOW, F32)] * 2)
            else:
                (a, la), (b, lb) = done[i, 0], done[i, 1]
                put(i, jnp.where(lane < 64, a, b).astype(BF), [la, lb])

    low = step * planes

    @pl.when(low > mine)
    def _():
        compute([2] * planes)

    @pl.when(low + planes - 1 < mine)
    def _():
        compute([0] * planes)

    for k in range(planes):

        @pl.when(low + k == mine)
        def _():
            compute([0] * k + [1] + [2] * (planes - 1 - k))


def attend(place, q8, near, far):
    planes, rows, _ = q8.shape
    each = 4
    whole = pl.BlockSpec(near.shape, lambda i, s: (0, 0, 0))
    return pl.pallas_call(
        attend_kernel,
        grid_spec=pltpu.PrefetchScalarGridSpec(
            num_scalar_prefetch=1,
            grid=(planes // each,),
            in_specs=[pl.BlockSpec((each, rows, 128), lambda i, s: (i, 0, 0)), whole, whole],
            out_specs=pl.BlockSpec((each, rows + 16, 128), lambda i, s: (i, 0, 0)),
            scratch_shapes=[pltpu.VMEM((8, rows, 256), BF)],
        ),
        out_shape=pltpu.HBM((planes, rows + 16, 128), BF),
        compiler_params=PARAMS,
        cost_estimate=SMALL,
        name="attend",
    )(place, q8, near, far)


def merge_kernel(o_ref, out_ref):
    planes = o_ref.shape[0]
    copies, rows, _ = out_ref.shape
    lane = lax.broadcasted_iota(jnp.int32, (128, 128), 1)
    for half in range(rows // 128):
        lses = []
        for i in range(planes):
            st = o_ref[i, rows : rows + 16, :].astype(F32)[8 * half : 8 * half + 6]
            lses.append(st[0:2] + st[2:4] + st[4:6])
        top = functools.reduce(jnp.maximum, lses)
        weights = [jnp.exp(v - top) for v in lses]
        total = functools.reduce(jnp.add, weights)
        pad = jnp.zeros((128 - 2 * planes, 128), F32)
        w = jnp.transpose(jnp.concatenate([v / total for v in weights] + [pad], axis=0))
        acc = 0.0
        for i in range(planes):
            wi = jnp.where(lane < 64, w[:, 2 * i : 2 * i + 1], w[:, 2 * i + 1 : 2 * i + 2])
            acc = acc + wi * o_ref[i, 128 * half : 128 * half + 128, :].astype(F32)
        for i in range(copies):
            out_ref[i, 128 * half : 128 * half + 128, :] = acc.astype(BF)


def merge(partial):
    rows = partial.shape[1] - 16
    return pl.pallas_call(
        merge_kernel,
        out_shape=pltpu.HBM((8, rows, 128), BF),
        in_specs=[VMEM],
        out_specs=VMEM,
        compiler_params=PARAMS,
        cost_estimate=SMALL,
        name="merge",
    )(partial)


def tail_kernel(place_ref, att_ref, x_ref, hw_ref, tgt_ref, *refs):
    near_refs, far_refs = refs[:4], refs[4:8]
    mixed_ref, stat_ref, a_s, m_s, f_s = refs[8:]
    parts, rows, width = x_ref.shape
    head, core = place_ref[0], place_ref[1]
    for i in range(parts):
        a_s[:, 128 * i : 128 * i + 128] = att_ref[place_ref[2 + i]]
    half = near_refs[0].shape[-1]
    for group, which in ((near_refs, core), (far_refs, 1 - core)):
        got = 0.0
        for k, ref in enumerate(group):
            w = ref[...].reshape(256, half)
            got = got + jnp.dot(a_s[:, 256 * k : 256 * k + 256], w, preferred_element_type=F32)
        m_s[:, pl.ds(pl.multiple_of(which * half, half), half)] = got.astype(BF)
    mixed_ref[...] = m_s[:, pl.ds(pl.multiple_of(head * width, width), width)]
    squares = 0.0
    for i in range(parts):
        resid = (x_ref[i].astype(F32) + m_s[:, i * width : (i + 1) * width].astype(F32)).astype(BF)
        wide = resid.astype(F32)
        squares = squares + jnp.sum(wide * wide, axis=-1, keepdims=True)
        f_s[:, i * width : (i + 1) * width] = resid
    r = lax.rsqrt(squares / (parts * width) + 1e-05)
    f_s[...] = (f_s[...].astype(F32) * r).astype(BF)
    final = f_s[...]
    books = tgt_ref.shape[1]
    share = hw_ref.shape[1] // 2
    lane = lax.broadcasted_iota(jnp.int32, (rows, 128), 1)
    stats = jnp.zeros((rows, 128), F32)
    for i in range(2):
        w = hw_ref[:, i * share : (i + 1) * share, :].reshape(parts * width, 256)
        both = jnp.dot(final, w, preferred_element_type=F32)
        for j in range(2):
            b = 2 * j + i
            logits = both[:, 128 * j : 128 * j + 128]
            g = jnp.max(logits, axis=-1, keepdims=True)
            s = jnp.sum(jnp.exp(logits - g), axis=-1, keepdims=True)
            hit = lane + 128 * head == tgt_ref[:, b : b + 1]
            picked = jnp.sum(jnp.where(hit, logits, 0.0), axis=-1, keepdims=True)
            stats = jnp.where(lane == b, g, stats)
            stats = jnp.where(lane == books + b, s, stats)
            stats = jnp.where(lane == 2 * books + b, picked, stats)
    stat_ref[...] = stats


def tail(place, att8, x8, hw, tgt, near, far):
    parts, rows, width = x8.shape
    return pl.pallas_call(
        tail_kernel,
        out_shape=(
            jax.ShapeDtypeStruct((rows, width), BF),
            jax.ShapeDtypeStruct((rows, 128), F32),
        ),
        in_specs=[SMEM] + [VMEM] * 12,
        out_specs=(VMEM, VMEM),
        scratch_shapes=[
            pltpu.VMEM((rows, parts * 128), BF),
            pltpu.VMEM((rows, parts * width), BF),
            pltpu.VMEM((rows, parts * width), BF),
        ],
        compiler_params=PARAMS,
        cost_estimate=SMALL,
        name="tail",
    )(place, att8, x8, hw, tgt, *near, *far)


def loss_kernel(s_ref, out_ref):
    books, share = out_ref.shape
    parts = s_ref.shape[0]
    top = s_ref[0]
    for i in range(1, parts):
        top = jnp.maximum(top, s_ref[i])
    total = 0.0
    picked = 0.0
    for i in range(parts):
        v = s_ref[i]
        total = total + jnp.exp(v - top) * pltpu.roll(v, 128 - books, 1)
        picked = picked + pltpu.roll(v, 128 - 2 * books, 1)
    loss = top + jnp.log(total) - picked
    full = jnp.concatenate([loss, jnp.zeros((128 - share, 128), F32)], axis=0)
    out_ref[...] = jnp.transpose(full)[:books, :share]


def final_loss(spread, books):
    return pl.pallas_call(
        loss_kernel,
        out_shape=jax.ShapeDtypeStruct((books, spread.shape[1]), F32),
        in_specs=[VMEM],
        out_specs=VMEM,
        cost_estimate=SMALL,
        name="loss",
    )(spread)


def shards(codes, delays, targets, embed, wqkv, wout, heads_w):
    books, rows = codes.shape
    vocab, width = embed.shape[1:]
    y, z, c = (lax.axis_index(a) for a in SEQ)
    x, h = (lax.axis_index(a) for a in HEAD)
    head = x * 2 + h
    slot = z * 2 + c
    first = (y * 8 + slot) * rows

    flat = heads_w.reshape(2, -1, heads_w.shape[-1])
    rows_here = jnp.concatenate([flat[0], flat[1]], axis=1)
    plane = trade(jnp.broadcast_to(rows_here[None], (8,) + rows_here.shape), ("z", "c"))
    devices = lax.axis_size(SEQ)
    behind = lax.ppermute(codes, SEQ, [(i, i + 1) for i in range(devices - 1)])
    w3 = jnp.transpose(wqkv, (1, 0, 2))

    columns = head * width + jnp.arange(width, dtype=jnp.int32)
    local = jnp.arange(rows, dtype=jnp.int32)
    frame_pos = first + local
    pos = lax.optimization_barrier(sinusoid(frame_pos.astype(F32), columns, width * 8))

    extended = jnp.concatenate([behind[:, rows - 3 :], codes], axis=1)
    ids = jnp.zeros((books, rows), jnp.int32)
    for d in range(4):
        ids = jnp.where(delays[:, None] == d, extended[:, 3 - d : 3 - d + rows], ids)
    ids = jnp.where(frame_pos[None, :] >= delays[:, None], ids, -1)
    hot = (jnp.transpose(ids)[:, :, None] == jnp.arange(vocab, dtype=jnp.int32)).astype(BF)
    summed = jnp.dot(
        hot.reshape(rows, books * vocab),
        embed.reshape(books * vocab, width),
        preferred_element_type=F32,
    )
    x_part = (summed + pos).astype(BF)
    x_part, plane = lax.optimization_barrier((x_part, plane))
    hw = lax.all_gather(plane, "y", axis=0).reshape((-1,) + rows_here.shape)

    other = flip(x_part, "h", 1)
    both = jnp.stack([jnp.where(h == 0, x_part, other), jnp.where(h == 0, other, x_part)])
    x8 = trade(jnp.broadcast_to(both[None], (4,) + both.shape), "x").reshape((8,) + x_part.shape)
    half = wout.shape[1] // 2
    mine = after(lax.dynamic_slice_in_dim(wout, c * half, half, 1), both)
    theirs = flip(mine, "h", 1)

    q, kv = project(x8, w3)
    q8 = trade(jnp.broadcast_to(q[None], (8,) + q.shape), "y")
    kv2 = jnp.stack([kv, flip(kv, "z", 2)])
    kv2 = after(kv2, theirs)
    kv4 = jnp.concatenate([kv2, flip(kv2, "z", 1)])
    kv4_far = flip(kv4, "c", 1)
    partial = attend(jnp.stack([y, slot]).astype(jnp.int32), q8, kv4, kv4_far)
    pair = jnp.stack(after([mine, theirs], q8))
    near = [pair] + [shift(pair, "x", k) for k in (1, 2, 3)]

    att = merge(trade(partial, "y"))
    waits = [partial] * 4
    far = [flip(after(n, first), "c", 1) for n, first in zip(near, waits)]
    att8 = trade(att, HEAD)

    order = [((x - k) % 4) * 2 + (h ^ j) for k in range(4) for j in range(2)]
    place = jnp.stack([head, c] + order).astype(jnp.int32)
    mixed, stats = tail(place, att8, x8, hw, jnp.transpose(targets), near, far)
    shares = trade(stats.reshape(8, rows // 8, 128), HEAD)
    return (mixed, final_loss(shares, books))


def solution(mesh):
    fine = Mesh(mesh.devices.reshape(8, 4, 2, 4, 2), SEQ + HEAD)
    placed = (
        P(None, SEQ),
        P(),
        P(None, SEQ),
        P(None, None, HEAD),
        P(None, None, HEAD),
        P(HEAD, None),
        P(None, SEQ, HEAD),
    )
    return jax.shard_map(
        shards,
        mesh=fine,
        in_specs=placed,
        out_specs=(P(SEQ, HEAD), P(None, SEQ + HEAD)),
        check_vma=False,
    )
```
